32 devices in a mesh: dom: 4 (over y, core), blk: 8 (over z, x).
Axes of the slice: x: 2, y: 2, z: 4, core: 2. Of those that a mesh axis runs over, the one named last changes fastest.
Arguments:
- particles: bfloat16 [1024, 9216], P(('dom', 'blk')), may hold values from -6 to 6
- references: bfloat16 [32, 9216], P('blk'), may hold values from -0.3 to 0.3
- inv_noise: float32 [1024], P(('dom', 'blk')), may hold values from 0.25 to 2
- significant: int32 [1024, 8], P(('dom', 'blk')), may hold values from 0 to 31, as said below
- sig_count: int32 [1024], P(('dom', 'blk')), may hold values from 2 to 8
Outputs:
- class_sums: float32 [32, 9216], P('blk', 'dom')
- class_weights: float32 [32], P('blk')
- log_evidence: float32 [1024], P(('dom', 'blk'))
The draws below stay inside these ranges and needn't reach their ends.
Inputs may be any that keep to these rules, and one draw needn't show every extreme that they name: `significant`: each row holds 8 class ids with distinct values of id // 4; in the rows of one device, at most 32 slots (used or not) name classes with the same id // 4, and some value is named exactly 32 times.
All inputs are finite; a program needn't handle non-finite values.
Results may differ from the reference program's by a relative error of at most 0.0025.
Values may be sent and summed in bfloat16 or wider, within the bound.
No kernel may reach another device: no remote copies, remote signals or barrier semaphores. Data moves between devices by JAX's collectives and lax.ppermute only.
A program may use at most 64 MiB of HBM per device.

```python
import math
import jax
import jax.numpy as jnp
from jax import lax

ROTS = 36
TOP = 8
CLS_DEV = 4
PART_DEV = 32
PIX = 9216
SHIFT = 256
K = 32
PARTICLES = 1024


def common_references(key):
    key = jax.random.fold_in(key, 101)
    return 0.05 * jnp.clip(jax.random.normal(key, (K, PIX), jnp.float32), -6.0, 6.0)


def common_lists(key):
    key = jax.random.fold_in(key, 202)
    key_perm, key_member = jax.random.split(key)
    owner_total = K // CLS_DEV
    block_total = PARTICLES // PART_DEV
    perm_keys = jax.random.split(key_perm, block_total)
    perms = jax.vmap(lambda one_key: jax.random.permutation(one_key, owner_total))(perm_keys).astype(jnp.int32)
    position = jnp.arange(PART_DEV * TOP, dtype=jnp.int32) % owner_total
    owners = perms[:, position].reshape(PARTICLES, TOP)
    members = jax.random.randint(key_member, (PARTICLES, TOP), 0, CLS_DEV).astype(jnp.int32)
    return (owners * CLS_DEV + members).astype(jnp.int32)


def common_inverse(key):
    key = jax.random.fold_in(key, 303)
    return jnp.exp(jax.random.uniform(key, (PARTICLES,), jnp.float32, math.log(0.25), math.log(2.0)))


def draw_references(key, part):
    return common_references(key).astype(jnp.bfloat16)


def draw_significant(key, part):
    return common_lists(key)


def draw_inv_noise(key, part):
    return common_inverse(key)


def draw_sig_count(key, part):
    key = jax.random.fold_in(key, 404)
    counts = jax.random.randint(key, (PARTICLES,), 2, TOP + 1).astype(jnp.int32)
    return counts.at[0].set(TOP).at[1].set(2)


def draw_particles(key, part):
    key = jax.random.fold_in(key, 505)
    key_noise = jax.random.fold_in(key, 0)
    result = jnp.clip(jax.random.normal(key_noise, (PARTICLES, PIX), jnp.float32), -6.0, 6.0)
    return result.astype(jnp.bfloat16)


def setup_inputs(seed: int = 0) -> dict:
    key_list = jax.random.split(jax.random.key(seed), 6)
    particles = draw_particles(jax.random.fold_in(key_list[5], 71), 0)
    references = draw_references(jax.random.fold_in(key_list[5], 71), 0)
    inv_noise = draw_inv_noise(jax.random.fold_in(key_list[5], 71), 0)
    significant = draw_significant(jax.random.fold_in(key_list[5], 71), 0)
    sig_count = draw_sig_count(jax.random.fold_in(key_list[5], 71), 0)
    return {"particles": particles, "references": references, "inv_noise": inv_noise, "significant": significant, "sig_count": sig_count}


def rotated_stack(images):
    batch = images.shape[0]
    pieces = images.reshape(batch, ROTS, SHIFT)
    turns = jnp.arange(ROTS, dtype=jnp.int32)
    source = (turns[:, None] + turns[None, :]) % ROTS
    return pieces[:, source, :].reshape(batch, ROTS, PIX)


def reference(particles, references, inv_noise, significant, sig_count):
    ref_wide = references.astype(jnp.float32)
    ref_norms = jnp.sum(ref_wide * ref_wide, axis=1)
    block_rows = math.gcd(PARTICLES, 64)
    groups = PARTICLES // block_rows
    slot_index = jnp.arange(TOP, dtype=jnp.int32)

    def visit(sums, inputs):
        images, inverse, class_ids, counts = inputs
        class_acc, weight_acc = sums
        rolled = rotated_stack(images.astype(jnp.float32))
        live_slot = slot_index[None, :] < counts[:, None]
        chosen = ref_wide[class_ids]
        corr = jnp.einsum("irp,isp->isr", rolled, chosen)
        scores = inverse[:, None, None] * (corr - 0.5 * ref_norms[class_ids][:, :, None])
        masked = jnp.where(live_slot[:, :, None], scores, -jnp.inf)
        row_peak = jnp.max(masked, axis=(1, 2))
        exp_terms = jnp.where(live_slot[:, :, None], jnp.exp(masked - row_peak[:, None, None]), 0.0)
        row_total = jnp.sum(exp_terms, axis=(1, 2))
        posterior = exp_terms / row_total[:, None, None]
        evidence = row_peak + jnp.log(row_total)
        rounded = lax.optimization_barrier(posterior.astype(jnp.bfloat16)).astype(jnp.float32)
        contrib = jnp.einsum("isr,irp->isp", rounded, rolled)
        target = jnp.where(live_slot, class_ids, K).astype(jnp.int32).reshape(-1)
        class_acc = class_acc + jax.ops.segment_sum(contrib.reshape(-1, PIX), target, num_segments=K + 1)[:K]
        weight_acc = weight_acc + jax.ops.segment_sum(jnp.sum(posterior, axis=2).reshape(-1), target, num_segments=K + 1)[:K]
        return (class_acc, weight_acc), evidence

    inputs = (particles.reshape(groups, block_rows, PIX), inv_noise.reshape(groups, block_rows),
              significant.reshape(groups, block_rows, TOP), sig_count.reshape(groups, block_rows))
    start_sums = (jnp.zeros((K, PIX), jnp.float32), jnp.zeros((K,), jnp.float32))
    (class_sums, class_weights), evidence = lax.scan(visit, start_sums, inputs)
    return class_sums, class_weights, evidence.reshape(PARTICLES)
```

```python
import functools
import jax
import jax.numpy as jnp
from jax import lax
from jax.experimental import pallas as pl
from jax.experimental.pallas import tpu as pltpu
from jax.sharding import PartitionSpec as P

ROTS = 36
LANES = 128
F32 = jnp.float32
BF16 = jnp.bfloat16
LOW = -3.0e38
VMEM_BYTES = 24 * 1024 * 1024


def offsets(blk):
    half = blk // 2
    first = [0] + list(range(half, blk - 2 + 1))
    second = [blk - 1] + list(range(half - 1, 0, -1))
    return first, second


def routed(block, dom, blk, move):
    pairs = []
    for d in range(dom):
        for b in range(blk):
            to = move(d, b)
            if to is not None:
                pairs.append((d * blk + b, to[0] * blk + to[1]))
    return lax.ppermute(block, ("dom", "blk"), pairs)


def in_vmem(count):
    return [pl.BlockSpec(memory_space=pltpu.VMEM)] * count


def call(kernel, outs, args, scratch=(), flops=1_000_000):
    total = sum(a.size * a.dtype.itemsize for a in args) + sum(o.size * o.dtype.itemsize for o in outs)
    return pl.pallas_call(
        kernel,
        out_shape=tuple(outs),
        in_specs=in_vmem(len(args)),
        out_specs=tuple(in_vmem(len(outs))),
        scratch_shapes=list(scratch),
        compiler_params=pltpu.CompilerParams(vmem_limit_bytes=VMEM_BYTES),
        cost_estimate=pl.CostEstimate(flops=flops, bytes_accessed=total, transcendentals=0),
    )(*args)


def stack_kernel(own, other, out):
    rows, pixels = own.shape
    step = pixels // ROTS
    for q in range(ROTS):
        base = q * 2 * rows
        out[base : base + rows, :] = own[:, q * step : (q + 1) * step]
        out[base + rows : base + 2 * rows, :] = other[:, q * step : (q + 1) * step]


def pick_offset(core, pair):
    return jnp.where(core == 0, pair[0], pair[1])


def lanes_of(own, other):
    return jnp.concatenate([own, other, own, other], axis=1)


def forward_kernel(pairs, slots, *refs):
    turns = len(pairs)
    own, recv, (stacked, small_own, small_other, exps, stats, tiles, acc) = refs[0], refs[1 : 1 + turns], refs[1 + turns :]
    core = lax.axis_index("dom") & 1
    spot = lax.axis_index("blk")
    width, pixels = own.shape
    step = pixels // ROTS
    total = stacked.shape[0]
    columns = total // LANES
    rows = ROTS * width
    norms = []
    for t in range(turns):
        block = recv[t][...].astype(F32)
        if t == 0:
            block = jnp.where(core == 0, own[...].astype(F32), block)
        norms.append(jnp.sum(block * block, axis=1, keepdims=True))
        for u in range(ROTS // 4):
            tile = jnp.concatenate([block[:, (4 * u + a) * step : (4 * u + a + 1) * step] for a in range(4)], axis=0)
            tiles[t * rows + 16 * u : t * rows + 16 * (u + 1), :] = tile.astype(BF16)
    acc[...] = jnp.zeros_like(acc)
    for n in range(columns // 2):
        weights = stacked[n * 256 : (n + 1) * 256, :]
        got = lax.dot_general(tiles[...], weights, (((1,), (1,)), ((), ())), preferred_element_type=F32)
        for t in range(turns):
            for m in range(-1, columns):
                part = None
                if m >= 0:
                    part = got[t * rows + 8 * m : t * rows + 8 * m + 8, :LANES]
                if m + 1 < columns:
                    extra = got[t * rows + 8 * m + 8 : t * rows + 8 * m + 16, LANES:]
                    part = extra if part is None else part + extra
                place = ((2 * n - m) % columns) * LANES
                acc[8 * t : 8 * t + 8, place : place + LANES] += part
    corr = []
    for t in range(turns):
        odd = pltpu.roll(acc[8 * t + 4 : 8 * t + 8, :], total - 64, 1)
        corr.append(acc[8 * t : 8 * t + 4, :] + odd)
    corr = jnp.concatenate(corr, axis=0)
    norm = jnp.concatenate(norms, axis=0)
    small = lanes_of(small_own[...], small_other[...])
    inverse = small[slots : slots + 1, :]
    ids = jnp.concatenate(
        [
            lax.broadcasted_iota(jnp.int32, (width, LANES), 0) + (spot ^ pick_offset(core, pair)) * width
            for pair in pairs
        ],
        axis=0,
    ).astype(F32)
    mask = small[0:1, :] == ids
    for s in range(1, slots):
        mask = mask | (small[s : s + 1, :] == ids)
    scores = [inverse * (corr[:, c * LANES : (c + 1) * LANES] - 0.5 * norm) for c in range(columns)]
    peak = jnp.full(ids.shape, LOW, F32)
    for score in scores:
        peak = jnp.maximum(peak, score)
    peak = jnp.max(jnp.where(mask, peak, LOW), axis=0, keepdims=True)
    peak = jnp.maximum(peak, pltpu.roll(peak, 64, 1))
    mass = jnp.zeros(ids.shape, F32)
    for c, score in enumerate(scores):
        term = jnp.where(mask, jnp.exp(score - peak), 0.0)
        exps[:, c * LANES : (c + 1) * LANES] = term
        mass = mass + term
    mass = jnp.sum(mass, axis=0, keepdims=True)
    mass = mass + pltpu.roll(mass, 64, 1)
    stats[...] = jnp.concatenate([peak, mass, jnp.zeros((6, LANES), F32)], axis=0)


def backward_kernel(turns, *refs):
    exps, mine, theirs, stacked = refs[:4]
    sends, (own, evidence, left) = refs[4 : 4 + turns], refs[4 + turns :]
    total = stacked.shape[0]
    columns = total // LANES
    width = exps.shape[0] // turns
    rows = ROTS * width
    extra_rows = own.shape[0] - rows
    peak, mass = mine[0:1, :], mine[1:2, :]
    peak_far, mass_far = pltpu.roll(theirs[0:1, :], 32, 1), pltpu.roll(theirs[1:2, :], 32, 1)
    top = jnp.maximum(peak, peak_far)
    share = jnp.exp(peak - top)
    whole = mass * share + mass_far * jnp.exp(peak_far - top)
    evidence[...] = (top + jnp.log(whole))[:, : evidence.shape[1]]
    factor = share / whole
    post = jnp.concatenate([exps[:, c * LANES : (c + 1) * LANES] * factor for c in range(columns)], axis=1)
    weight = jnp.sum(post, axis=1, keepdims=True)
    turned = pltpu.roll(post, 64, 1)
    for t in range(turns):
        two = jnp.concatenate([post[width * t : width * (t + 1), :], turned[width * t : width * (t + 1), :]], axis=0)
        four = jnp.concatenate([two, pltpu.roll(two, 128, 1)], axis=0).astype(BF16)
        for u in range(ROTS // 4):
            cut = total - 256 * u
            rotated = four if u == 0 else jnp.concatenate([four[:, cut:], four[:, :cut]], axis=1)
            left[t * rows + 16 * u : t * rows + 16 * (u + 1), :] = rotated
    result = jnp.dot(left[...], stacked[...], preferred_element_type=F32)
    lane = lax.broadcasted_iota(jnp.int32, (extra_rows, own.shape[1]), 1)
    row = lax.broadcasted_iota(jnp.int32, (extra_rows, own.shape[1]), 0)
    for t in range(turns):
        piece = weight[width * t : width * (t + 1), :]
        piece = jnp.concatenate([piece, jnp.zeros((extra_rows - width, 1), F32)], axis=0)
        block = result[t * rows : (t + 1) * rows, :]
        high = piece.astype(BF16).astype(F32)
        middle = (piece - high).astype(BF16).astype(F32)
        low = piece - high - middle
        if t == 0:
            own[:rows, :] = block
            own[rows:, :] = jnp.where(lane == 0, piece, 0.0)
        sends[t][:rows, :] = block.astype(BF16)
        sends[t][rows:, :] = jnp.where(
            lane == 0, high, jnp.where(lane == 1, middle, jnp.where(lane == 2, low, 0.0))
        ).astype(BF16)


def gather_kernel(turns, width, *refs):
    own, recv, outs, split = refs[0], refs[1 : 1 + turns], refs[1 + turns : -1], refs[-1]
    shards = len(outs)
    me = lax.axis_index("dom")
    rows = ROTS * width
    part = rows // shards
    value = recv[0][...].astype(F32)
    value = jnp.where((me & 1) == 0, own[...], value)
    for t in range(1, turns):
        value = value + recv[t][...].astype(F32)
    weight = jnp.sum(value[rows : rows + width, :], axis=1, keepdims=True)
    weight = jnp.broadcast_to(weight, (width, value.shape[1]))
    for s in range(shards):
        split[s, :, :] = jnp.concatenate([value[s * part : (s + 1) * part, :], weight], axis=0)
    for s in range(shards):
        outs[s][...] = split[me ^ s]


def finish_kernel(width, *refs):
    parts, (sums, weights) = refs[:-2], refs[-2:]
    value = parts[0][...]
    for part in parts[1:]:
        value = value + part[...]
    step = value.shape[1]
    chunks = value.shape[0] // width - 1
    for c in range(chunks):
        sums[:, c * step : (c + 1) * step] = value[c * width : (c + 1) * width, :]
    tail = value[chunks * width :, :LANES]
    pick = lax.broadcasted_iota(jnp.int32, tail.shape, 0) == lax.broadcasted_iota(jnp.int32, tail.shape, 1)
    weights[...] = jnp.sum(jnp.where(pick, tail, 0.0), axis=0, keepdims=True)[:, : weights.shape[1]]


def body(particles, references, inv_noise, significant, sig_count):
    dom, blk = lax.axis_size("dom"), lax.axis_size("blk")
    count, pixels = particles.shape
    width = references.shape[0]
    slots = significant.shape[1]
    step = pixels // ROTS
    first, second = offsets(blk)
    pairs = list(zip(first, second))
    turns = len(pairs)
    total = ROTS * 2 * count
    shape = jax.ShapeDtypeStruct

    def over_blk(block, pair):
        def move(d, b):
            by = pair[d & 1]
            return None if by == 0 else (d, b ^ by)

        return routed(block, dom, blk, move)

    def over_dom(block, by):
        return routed(block, dom, blk, lambda d, b: (d ^ by, b))

    recv = [over_blk(references, pair) for pair in pairs]
    other = over_dom(particles, 1)
    live = lax.broadcasted_iota(jnp.int32, (slots, count), 0) < sig_count[None, :]
    small = jnp.concatenate(
        [
            jnp.where(live, significant.T, -1).astype(F32),
            inv_noise[None, :],
            jnp.zeros((7, count), F32),
        ],
        axis=0,
    )
    small_other = over_dom(small, 1)
    (stacked,) = call(stack_kernel, [shape((total, step), BF16)], [particles, other])
    exps, stats = call(
        functools.partial(forward_kernel, pairs, slots),
        [shape((turns * width, total), F32), shape((8, LANES), F32)],
        [references, *recv, stacked, small, small_other],
        [pltpu.VMEM((turns * ROTS * width, step), BF16), pltpu.VMEM((turns * 8, total), F32)],
    )
    stats_other = over_dom(stats, 1)
    rows = ROTS * width
    *sends, own, evidence = call(
        functools.partial(backward_kernel, turns),
        [shape((rows + 16, step), BF16)] * turns + [shape((rows + 16, step), F32), shape((1, count), F32)],
        [exps, stats, stats_other, stacked],
        [pltpu.VMEM((turns * rows, total), BF16)],
    )
    recv = [over_blk(block, pair) for block, pair in zip(sends, pairs)]
    parts = call(
        functools.partial(gather_kernel, turns, width),
        [shape((rows // dom + width, step), F32)] * dom,
        [own, *recv],
        [pltpu.VMEM((dom, rows // dom + width, step), F32)],
    )
    parts = [parts[0]] + [over_dom(parts[s], s) for s in range(1, dom)]
    sums, weights = call(
        functools.partial(finish_kernel, width),
        [shape((width, pixels // dom), F32), shape((1, width), F32)],
        parts,
    )
    return sums, weights.reshape(width), evidence.reshape(count)


def solution(mesh):
    in_specs = (
        P(("dom", "blk"), None),
        P("blk", None),
        P(("dom", "blk")),
        P(("dom", "blk"), None),
        P(("dom", "blk")),
    )
    out_specs = (P("blk", "dom"), P("blk"), P(("dom", "blk")))
    return jax.shard_map(body, mesh=mesh, in_specs=in_specs, out_specs=out_specs, check_vma=False)
```

```python
import functools
import jax
import jax.numpy as jnp
from jax import lax
from jax.experimental import pallas as pl
from jax.experimental.pallas import tpu as pltpu
from jax.sharding import PartitionSpec as P

ROTS = 36
LANES = 128
F32 = jnp.float32
BF16 = jnp.bfloat16
LOW = -3.0e38
VMEM_BYTES = 24 * 1024 * 1024


def offsets(blk):
    half = blk // 2
    first = list(range(half, blk - 1)) + [0]
    second = [blk - 1] + list(range(half - 1, 0, -1))
    pairs = list(zip(first, second))
    order = list(range(1, half)) + [0]
    return pairs, order


def routed(block, dom, blk, move):
    pairs = []
    for d in range(dom):
        for b in range(blk):
            to = move(d, b)
            if to is not None:
                pairs.append((d * blk + b, to[0] * blk + to[1]))
    return lax.ppermute(block, ("dom", "blk"), pairs)


def call(kernel, outs, args, scratch=(), flops=1_000_000):
    total = sum(a.size * a.dtype.itemsize for a in args) + sum(o.size * o.dtype.itemsize for o in outs)
    near = pl.BlockSpec(memory_space=pltpu.VMEM)
    return pl.pallas_call(
        kernel,
        out_shape=tuple(outs),
        in_specs=[near] * len(args),
        out_specs=tuple([near] * len(outs)),
        scratch_shapes=list(scratch),
        compiler_params=pltpu.CompilerParams(vmem_limit_bytes=VMEM_BYTES),
        cost_estimate=pl.CostEstimate(flops=flops, bytes_accessed=total, transcendentals=0),
    )(*args)


def stack_kernel(own, other, out):
    rows, pixels = own.shape
    step = pixels // ROTS
    for q in range(ROTS):
        base = q * 2 * rows
        out[base : base + rows, :] = own[:, q * step : (q + 1) * step]
        out[base + rows : base + 2 * rows, :] = other[:, q * step : (q + 1) * step]


def pick_offset(core, pair):
    return jnp.where(core == 0, pair[0], pair[1])


def lanes_of(own, other):
    return jnp.concatenate([own, other, own, other], axis=1)


def forward_kernel(pairs, *refs):
    turns = len(pairs)
    recv = refs[:turns]
    stacked, lists_own, lists_other, exps, stats, tiles, acc = refs[turns:]
    core = lax.axis_index("dom") & 1
    spot = lax.axis_index("blk")
    width, pixels = recv[0].shape
    slots = lists_own.shape[0] // 2
    lists = lanes_of(lists_own[...], lists_other[...])
    step = pixels // ROTS
    total = stacked.shape[0]
    columns = total // LANES
    rows = ROTS * width
    norms = []
    for t in range(turns):
        block = recv[t][...].astype(F32)
        norms.append(jnp.sum(block * block, axis=1, keepdims=True))
        for u in range(ROTS // 4):
            tile = jnp.concatenate([block[:, (4 * u + a) * step : (4 * u + a + 1) * step] for a in range(4)], axis=0)
            tiles[t * rows + 16 * u : t * rows + 16 * (u + 1), :] = tile.astype(BF16)
    acc[...] = jnp.zeros_like(acc)
    for n in range(columns // 2):
        weights = stacked[n * 256 : (n + 1) * 256, :]
        got = lax.dot_general(tiles[...], weights, (((1,), (1,)), ((), ())), preferred_element_type=F32)
        for t in range(turns):
            for m in range(-1, columns):
                part = None
                if m >= 0:
                    part = got[t * rows + 8 * m : t * rows + 8 * m + 8, :LANES]
                if m + 1 < columns:
                    extra = got[t * rows + 8 * m + 8 : t * rows + 8 * m + 16, LANES:]
                    part = extra if part is None else part + extra
                place = ((2 * n - m) % columns) * LANES
                acc[8 * t : 8 * t + 8, place : place + LANES] += part
    corr = []
    for t in range(turns):
        odd = pltpu.roll(acc[8 * t + 4 : 8 * t + 8, :], total - 64, 1)
        corr.append(acc[8 * t : 8 * t + 4, :] + odd)
    corr = jnp.concatenate(corr, axis=0)
    norm = jnp.concatenate(norms, axis=0)
    inverse = lists[slots : slots + 1, :]
    ids = jnp.concatenate(
        [
            lax.broadcasted_iota(jnp.int32, (width, LANES), 0) + (spot ^ pick_offset(core, pair)) * width
            for pair in pairs
        ],
        axis=0,
    ).astype(F32)
    mask = lists[0:1, :] == ids
    for s in range(1, slots):
        mask = mask | (lists[s : s + 1, :] == ids)
    scores = [inverse * (corr[:, c * LANES : (c + 1) * LANES] - 0.5 * norm) for c in range(columns)]
    peak = jnp.full(ids.shape, LOW, F32)
    for score in scores:
        peak = jnp.maximum(peak, score)
    peak = jnp.max(jnp.where(mask, peak, LOW), axis=0, keepdims=True)
    peak = jnp.maximum(peak, pltpu.roll(peak, 64, 1))
    mass = jnp.zeros(ids.shape, F32)
    for c, score in enumerate(scores):
        term = jnp.where(mask, jnp.exp(score - peak), 0.0)
        exps[:, c * LANES : (c + 1) * LANES] = term
        mass = mass + term
    mass = jnp.sum(mass, axis=0, keepdims=True)
    mass = mass + pltpu.roll(mass, 64, 1)
    stats[...] = jnp.concatenate([peak, mass, jnp.zeros((6, LANES), F32)], axis=0)


def backward_kernel(pairs, *refs):
    turns = len(pairs)
    exps, mine, theirs, stacked = refs[:4]
    sends, (own, evidence, left) = refs[4 : 4 + turns], refs[4 + turns :]
    total = stacked.shape[0]
    columns = total // LANES
    width = exps.shape[0] // turns
    rows = ROTS * width
    extra_rows = own.shape[0] - rows
    peak, mass = mine[0:1, :], mine[1:2, :]
    peak_far, mass_far = pltpu.roll(theirs[0:1, :], 32, 1), pltpu.roll(theirs[1:2, :], 32, 1)
    top = jnp.maximum(peak, peak_far)
    share = jnp.exp(peak - top)
    whole = mass * share + mass_far * jnp.exp(peak_far - top)
    evidence[...] = (top + jnp.log(whole))[:, : evidence.shape[1]]
    factor = share / whole
    post = jnp.concatenate([exps[:, c * LANES : (c + 1) * LANES] * factor for c in range(columns)], axis=1)
    weight = jnp.sum(post, axis=1, keepdims=True)
    turned = pltpu.roll(post, 64, 1)
    for t in range(turns):
        two = jnp.concatenate([post[width * t : width * (t + 1), :], turned[width * t : width * (t + 1), :]], axis=0)
        four = jnp.concatenate([two, pltpu.roll(two, 128, 1)], axis=0).astype(BF16)
        for u in range(ROTS // 4):
            cut = total - 256 * u
            rotated = four if u == 0 else jnp.concatenate([four[:, cut:], four[:, :cut]], axis=1)
            left[t * rows + 16 * u : t * rows + 16 * (u + 1), :] = rotated
    result = jnp.dot(left[...], stacked[...], preferred_element_type=F32)
    lane = lax.broadcasted_iota(jnp.int32, (extra_rows, own.shape[1]), 1)
    row = lax.broadcasted_iota(jnp.int32, (extra_rows, own.shape[1]), 0)
    for t in range(turns):
        piece = weight[width * t : width * (t + 1), :]
        piece = jnp.concatenate([piece, jnp.zeros((extra_rows - width, 1), F32)], axis=0)
        block = result[t * rows : (t + 1) * rows, :]
        high = piece.astype(BF16).astype(F32)
        middle = (piece - high).astype(BF16).astype(F32)
        low = piece - high - middle
        if pairs[t][0] == 0:
            own[:rows, :] = block
            own[rows:, :] = jnp.where(lane == 0, piece, 0.0)
        tail = jnp.where(lane == 0, high, jnp.where(lane == 1, middle, jnp.where(lane == 2, low, 0.0)))
        sends[t][...] = jnp.concatenate([block, tail], axis=0).astype(BF16)


def gather_kernel(pairs, width, *refs):
    turns = len(pairs)
    own, recv, (keep, give) = refs[0], refs[1 : 1 + turns], refs[1 + turns :]
    core = lax.axis_index("dom") & 1
    rows = ROTS * width
    sides = keep.shape[0]
    part = rows // (2 * sides)
    value = None
    for t in range(turns):
        block = recv[t][...].astype(F32)
        if pairs[t][0] == 0:
            block = jnp.where(core == 0, own[...], block)
        value = block if value is None else value + block
    weight = jnp.sum(value[rows : rows + width, :], axis=1, keepdims=True)
    weight = jnp.broadcast_to(weight, (width, value.shape[1]))
    for s in range(sides):
        one = value[2 * s * part : (2 * s + 1) * part, :]
        two = value[(2 * s + 1) * part : (2 * s + 2) * part, :]
        keep[s, :, :] = jnp.concatenate([jnp.where(core == 0, one, two), weight], axis=0)
        give[s, :, :] = jnp.concatenate([jnp.where(core == 0, two, one), weight], axis=0)


def pair_kernel(keep, given, *refs):
    outs, both = refs[:-1], refs[-1]
    side = lax.axis_index("dom") >> 1
    both[...] = keep[...] + given[...]
    for s, out in enumerate(outs):
        out[...] = both[side ^ s]


def finish_kernel(width, *refs):
    parts, (sums, weights) = refs[:-2], refs[-2:]
    value = parts[0][...]
    for part in parts[1:]:
        value = value + part[...]
    step = value.shape[1]
    chunks = value.shape[0] // width - 1
    for c in range(chunks):
        sums[:, c * step : (c + 1) * step] = value[c * width : (c + 1) * width, :]
    tail = value[chunks * width :, :LANES]
    pick = lax.broadcasted_iota(jnp.int32, tail.shape, 0) == lax.broadcasted_iota(jnp.int32, tail.shape, 1)
    weights[...] = jnp.sum(jnp.where(pick, tail, 0.0), axis=0, keepdims=True)[:, : weights.shape[1]]


def body(particles, references, inv_noise, significant, sig_count):
    dom, blk = lax.axis_size("dom"), lax.axis_size("blk")
    count, pixels = particles.shape
    width = references.shape[0]
    slots = significant.shape[1]
    step = pixels // ROTS
    pairs, order = offsets(blk)
    turns = len(pairs)
    total = ROTS * 2 * count
    shape = jax.ShapeDtypeStruct

    def over_blk(block, pair):
        def move(d, b):
            by = pair[d & 1]
            return None if by == 0 else (d, b ^ by)

        return routed(block, dom, blk, move)

    def shared(block, pair):
        def move(d, b):
            if pair[0] != 0:
                return (d, b ^ pair[d & 1])
            return (d ^ 1, b) if d & 1 else (d ^ 1, b ^ pair[1])

        return routed(block, dom, blk, move)

    def over_dom(block, by):
        return routed(block, dom, blk, lambda d, b: (d ^ by, b))

    other = over_dom(particles, 1)
    row = lax.broadcasted_iota(jnp.int32, (2 * slots, count), 0)
    named = jnp.pad(significant.T, ((0, slots), (0, 0)))
    named = jnp.where(row < sig_count[None, :], named, -1).astype(F32)
    lists = jnp.where(row < slots, named, inv_noise[None, :])
    recv = [shared(references, pair) for pair in pairs]
    lists_other = over_dom(lists, 1)
    (stacked,) = call(stack_kernel, [shape((total, step), BF16)], [particles, other])
    exps, stats = call(
        functools.partial(forward_kernel, pairs),
        [shape((turns * width, total), F32), shape((8, LANES), F32)],
        [*recv, stacked, lists, lists_other],
        [pltpu.VMEM((turns * ROTS * width, step), BF16), pltpu.VMEM((turns * 8, total), F32)],
    )
    stats_other = over_dom(stats, 1)
    rows = ROTS * width
    *sends, own, evidence = call(
        functools.partial(backward_kernel, pairs),
        [shape((rows + 8, step), BF16)] * turns + [shape((rows + 8, step), F32), shape((1, count), F32)],
        [exps, stats, stats_other, stacked],
        [pltpu.VMEM((turns * rows, total), BF16)],
    )
    recv = [over_blk(sends[t], pairs[t]) for t in order]
    sides, part = dom // 2, rows // dom + width
    keep, give = call(
        functools.partial(gather_kernel, [pairs[t] for t in order], width),
        [shape((sides, part, step), F32)] * 2,
        [own, *recv],
    )
    parts = call(
        pair_kernel,
        [shape((part, step), F32)] * sides,
        [keep, over_dom(give, 1)],
        [pltpu.VMEM((sides, part, step), F32)],
    )
    parts = [parts[0]] + [over_dom(parts[s], 2 * s) for s in range(1, sides)]
    sums, weights = call(
        functools.partial(finish_kernel, width),
        [shape((width, pixels // dom), F32), shape((1, width), F32)],
        parts,
    )
    return sums, weights.reshape(width), evidence.reshape(count)


def solution(mesh):
    in_specs = (
        P(("dom", "blk"), None),
        P("blk", None),
        P(("dom", "blk")),
        P(("dom", "blk"), None),
        P(("dom", "blk")),
    )
    out_specs = (P("blk", "dom"), P("blk"), P(("dom", "blk")))
    return jax.shard_map(body, mesh=mesh, in_specs=in_specs, out_specs=out_specs, check_vma=False)
```

```python
import functools
import jax
import jax.numpy as jnp
from jax import lax
from jax.experimental import pallas as pl
from jax.experimental.pallas import tpu as pltpu
from jax.sharding import PartitionSpec as P

ROTS = 36
LANES = 128
F32 = jnp.float32
BF16 = jnp.bfloat16
LOW = -3.0e38
VMEM_BYTES = 24 * 1024 * 1024


def offsets(blk):
    half = blk // 2
    first = list(range(half, blk - 1)) + [0]
    second = [blk - 1] + list(range(half - 1, 0, -1))
    pairs = list(zip(first, second))
    order = list(range(1, half)) + [0]
    return pairs, order


def routed(block, dom, blk, move):
    pairs = []
    for d in range(dom):
        for b in range(blk):
            to = move(d, b)
            if to is not None:
                pairs.append((d * blk + b, to[0] * blk + to[1]))
    return lax.ppermute(block, ("dom", "blk"), pairs)


def call(kernel, outs, args, scratch=(), flops=1_000_000):
    total = sum(a.size * a.dtype.itemsize for a in args) + sum(o.size * o.dtype.itemsize for o in outs)
    near = pl.BlockSpec(memory_space=pltpu.VMEM)
    return pl.pallas_call(
        kernel,
        out_shape=tuple(outs),
        in_specs=[near] * len(args),
        out_specs=tuple([near] * len(outs)),
        scratch_shapes=list(scratch),
        compiler_params=pltpu.CompilerParams(vmem_limit_bytes=VMEM_BYTES),
        cost_estimate=pl.CostEstimate(flops=flops, bytes_accessed=total, transcendentals=0),
    )(*args)


def stack_kernel(own, other, out):
    rows, pixels = own.shape
    step = pixels // ROTS
    for q in range(ROTS):
        base = q * 2 * rows
        out[base : base + rows, :] = own[:, q * step : (q + 1) * step]
        out[base + rows : base + 2 * rows, :] = other[:, q * step : (q + 1) * step]


def pick_offset(core, pair):
    return jnp.where(core == 0, pair[0], pair[1])


def lanes_of(own, other):
    return jnp.concatenate([own, other, own, other], axis=1)


def correlate(recv, stacked, tiles):
    width, pixels = recv[0].shape
    step = pixels // ROTS
    total = stacked.shape[0]
    columns = total // LANES
    rows = ROTS * width
    norms = []
    for t, ref in enumerate(recv):
        block = ref[...].astype(F32)
        norms.append(0.5 * jnp.sum(block * block, axis=1, keepdims=True))
        for u in range(ROTS // 4):
            tile = jnp.concatenate([block[:, (4 * u + a) * step : (4 * u + a + 1) * step] for a in range(4)], axis=0)
            tiles[t * rows + 16 * u : t * rows + 16 * (u + 1), :] = tile.astype(BF16)
    sums = [[None] * columns for _ in recv]
    for n in range(columns // 2):
        weights = stacked[n * 256 : (n + 1) * 256, :]
        got = lax.dot_general(tiles[...], weights, (((1,), (1,)), ((), ())), preferred_element_type=F32)
        for t, held in enumerate(sums):
            for m in range(-1, columns):
                part = None
                if m >= 0:
                    part = got[t * rows + 8 * m : t * rows + 8 * m + 8, :LANES]
                if m + 1 < columns:
                    extra = got[t * rows + 8 * m + 8 : t * rows + 8 * m + 16, LANES:]
                    part = extra if part is None else part + extra
                place = (2 * n - m) % columns
                held[place] = part if held[place] is None else held[place] + part
    corr = []
    for held in sums:
        whole = jnp.concatenate(held, axis=1)
        corr.append(whole[:4, :] + pltpu.roll(whole, total - 64, 1)[4:, :])
    return jnp.concatenate(corr, axis=0), jnp.concatenate(norms, axis=0)


def early_kernel(*refs):
    recv, (stacked, corr, norm, tiles) = refs[:-4], refs[-4:]
    value, norms = correlate(recv, stacked, tiles)
    corr[...] = value
    norm[...] = jnp.broadcast_to(norms, norm.shape)


def forward_kernel(pairs, *refs):
    recv, (stacked, lists_own, lists_other) = refs[:-9], refs[-9:-6]
    early, early_norm, exps, stats, tiles, corr = refs[-6:]
    core = lax.axis_index("dom") & 1
    spot = lax.axis_index("blk")
    width = recv[0].shape[0]
    slots = lists_own.shape[0] // 2
    columns = stacked.shape[0] // LANES
    late, late_norm = correlate(recv, stacked, tiles)
    corr[: early.shape[0], :] = early[...]
    corr[early.shape[0] :, :] = late
    norm = jnp.concatenate([early_norm[...], jnp.broadcast_to(late_norm, (late_norm.shape[0], LANES))], axis=0)
    lists = lanes_of(lists_own[...], lists_other[...])
    inverse = lists[slots : slots + 1, :]
    ids = jnp.concatenate(
        [
            lax.broadcasted_iota(jnp.int32, (width, LANES), 0) + (spot ^ pick_offset(core, pair)) * width
            for pair in pairs
        ],
        axis=0,
    ).astype(F32)
    mask = lists[0:1, :] == ids
    for s in range(1, slots):
        mask = mask | (lists[s : s + 1, :] == ids)
    scores = [inverse * (corr[:, c * LANES : (c + 1) * LANES] - norm) for c in range(columns)]
    peak = jnp.full(ids.shape, LOW, F32)
    for score in scores:
        peak = jnp.maximum(peak, score)
    peak = jnp.max(jnp.where(mask, peak, LOW), axis=0, keepdims=True)
    peak = jnp.maximum(peak, pltpu.roll(peak, 64, 1))
    mass = jnp.zeros(ids.shape, F32)
    for c, score in enumerate(scores):
        term = jnp.where(mask, jnp.exp(score - peak), 0.0)
        exps[:, c * LANES : (c + 1) * LANES] = term
        mass = mass + term
    mass = jnp.sum(mass, axis=0, keepdims=True)
    mass = mass + pltpu.roll(mass, 64, 1)
    stats[...] = jnp.concatenate([peak, mass, jnp.zeros((6, LANES), F32)], axis=0)


def backward_kernel(pairs, *refs):
    taken = range(len(pairs))
    exps, mine, theirs, stacked = refs[:4]
    sends, (own, evidence, left) = refs[4:-3], refs[-3:]
    total = stacked.shape[0]
    columns = total // LANES
    width = exps.shape[0] // len(pairs)
    rows = ROTS * width
    extra_rows, step = sends[0].shape[0] - rows, sends[0].shape[1]
    peak, mass = mine[0:1, :], mine[1:2, :]
    peak_far, mass_far = pltpu.roll(theirs[0:1, :], 32, 1), pltpu.roll(theirs[1:2, :], 32, 1)
    top = jnp.maximum(peak, peak_far)
    share = jnp.exp(peak - top)
    whole = mass * share + mass_far * jnp.exp(peak_far - top)
    factor = share / whole
    evidence[...] = (top + jnp.log(whole))[:, : evidence.shape[1]]
    weights = []
    for n, t in enumerate(taken):
        post = jnp.concatenate(
            [exps[width * t : width * (t + 1), c * LANES : (c + 1) * LANES] * factor for c in range(columns)], axis=1
        )
        weights.append(jnp.sum(post, axis=1, keepdims=True))
        two = jnp.concatenate([post, pltpu.roll(post, 64, 1)], axis=0)
        four = jnp.concatenate([two, pltpu.roll(two, 128, 1)], axis=0).astype(BF16)
        for u in range(ROTS // 4):
            cut = total - 256 * u
            rotated = four if u == 0 else jnp.concatenate([four[:, cut:], four[:, :cut]], axis=1)
            left[n * rows + 16 * u : n * rows + 16 * (u + 1), :] = rotated
    result = jnp.dot(left[...], stacked[...], preferred_element_type=F32)
    lane = lax.broadcasted_iota(jnp.int32, (extra_rows, step), 1)
    for n, t in enumerate(taken):
        piece = jnp.concatenate([weights[n], jnp.zeros((extra_rows - width, 1), F32)], axis=0)
        block = result[n * rows : (n + 1) * rows, :]
        high = piece.astype(BF16).astype(F32)
        middle = (piece - high).astype(BF16).astype(F32)
        low = piece - high - middle
        if pairs[t][0] == 0:
            own[:rows, :] = block
            own[rows:, :] = jnp.where(lane == 0, piece, 0.0)
        tail = jnp.where(lane == 0, high, jnp.where(lane == 1, middle, jnp.where(lane == 2, low, 0.0)))
        sends[n][...] = jnp.concatenate([block, tail], axis=0).astype(BF16)


def gather_kernel(pairs, width, *refs):
    turns = len(pairs)
    own, recv, (keep, give) = refs[0], refs[1 : 1 + turns], refs[1 + turns :]
    core = lax.axis_index("dom") & 1
    rows = ROTS * width
    sides = keep.shape[0]
    part = rows // (2 * sides)
    value = None
    for t in range(turns):
        block = recv[t][...].astype(F32)
        if pairs[t][0] == 0:
            block = jnp.where(core == 0, own[...], block)
        value = block if value is None else value + block
    weight = jnp.sum(value[rows : rows + width, :], axis=1, keepdims=True)
    weight = jnp.broadcast_to(weight, (width, value.shape[1]))
    for s in range(sides):
        one = value[2 * s * part : (2 * s + 1) * part, :]
        two = value[(2 * s + 1) * part : (2 * s + 2) * part, :]
        keep[s, :, :] = jnp.concatenate([jnp.where(core == 0, one, two), weight], axis=0)
        give[s, :, :] = jnp.concatenate([jnp.where(core == 0, two, one), weight], axis=0)


def pair_kernel(keep, given, *refs):
    outs, both = refs[:-1], refs[-1]
    side = lax.axis_index("dom") >> 1
    both[...] = keep[...] + given[...]
    for s, out in enumerate(outs):
        out[...] = both[side ^ s]


def finish_kernel(width, *refs):
    parts, (sums, weights) = refs[:-2], refs[-2:]
    value = parts[0][...]
    for part in parts[1:]:
        value = value + part[...]
    step = value.shape[1]
    chunks = value.shape[0] // width - 1
    for c in range(chunks):
        sums[:, c * step : (c + 1) * step] = value[c * width : (c + 1) * width, :]
    tail = value[chunks * width :, :LANES]
    pick = lax.broadcasted_iota(jnp.int32, tail.shape, 0) == lax.broadcasted_iota(jnp.int32, tail.shape, 1)
    weights[...] = jnp.sum(jnp.where(pick, tail, 0.0), axis=0, keepdims=True)[:, : weights.shape[1]]


def body(particles, references, inv_noise, significant, sig_count):
    dom, blk = lax.axis_size("dom"), lax.axis_size("blk")
    count, pixels = particles.shape
    width = references.shape[0]
    slots = significant.shape[1]
    step = pixels // ROTS
    pairs, order = offsets(blk)
    turns = len(pairs)
    total = ROTS * 2 * count
    shape = jax.ShapeDtypeStruct

    def over_blk(block, pair):
        def move(d, b):
            by = pair[d & 1]
            return None if by == 0 else (d, b ^ by)

        return routed(block, dom, blk, move)

    def shared(block, pair):
        def move(d, b):
            if pair[0] != 0:
                return (d, b ^ pair[d & 1])
            return (d ^ 1, b) if d & 1 else (d ^ 1, b ^ pair[1])

        return routed(block, dom, blk, move)

    def over_dom(block, by):
        return routed(block, dom, blk, lambda d, b: (d ^ by, b))

    other = over_dom(particles, 1)
    row = lax.broadcasted_iota(jnp.int32, (2 * slots, count), 0)
    named = jnp.pad(significant.T, ((0, slots), (0, 0)))
    named = jnp.where(row < sig_count[None, :], named, -1).astype(F32)
    lists = jnp.where(row < slots, named, inv_noise[None, :])
    recv = [shared(references, pair) for pair in pairs]
    lists_other = over_dom(lists, 1)
    (stacked,) = call(stack_kernel, [shape((total, step), BF16)], [particles, other])
    rows = ROTS * width

    def buffers(blocks):
        return [pltpu.VMEM((blocks * rows, step), BF16)]

    early = turns // 2
    corr, norm = call(
        early_kernel,
        [shape((early * width, total), F32), shape((early * width, LANES), F32)],
        [*recv[:early], stacked],
        buffers(early),
        flops=2 * early * rows * step * total,
    )
    exps, stats = call(
        functools.partial(forward_kernel, pairs),
        [shape((turns * width, total), F32), shape((8, LANES), F32)],
        [*recv[early:], stacked, lists, lists_other, corr, norm],
        buffers(turns - early) + [pltpu.VMEM((turns * width, total), F32)],
        flops=2 * (turns - early) * rows * step * total,
    )
    stats_other = over_dom(stats, 1)
    message = shape((rows + 8, step), BF16)
    *sends, own, evidence = call(
        functools.partial(backward_kernel, pairs),
        [message] * turns + [shape((rows + 8, step), F32), shape((1, count), F32)],
        [exps, stats, stats_other, stacked],
        [pltpu.VMEM((turns * rows, total), BF16)],
        flops=2 * turns * rows * step * total,
    )
    recv = [over_blk(sends[t], pairs[t]) for t in order]
    sides, part = dom // 2, rows // dom + width
    keep, give = call(
        functools.partial(gather_kernel, [pairs[t] for t in order], width),
        [shape((sides, part, step), F32)] * 2,
        [own, *recv],
    )
    parts = call(
        pair_kernel,
        [shape((part, step), F32)] * sides,
        [keep, over_dom(give, 1)],
        [pltpu.VMEM((sides, part, step), F32)],
    )
    parts = [parts[0]] + [over_dom(parts[s], 2 * s) for s in range(1, sides)]
    sums, weights = call(
        functools.partial(finish_kernel, width),
        [shape((width, pixels // dom), F32), shape((1, width), F32)],
        parts,
    )
    return sums, weights.reshape(width), evidence.reshape(count)


def solution(mesh):
    in_specs = (
        P(("dom", "blk"), None),
        P("blk", None),
        P(("dom", "blk")),
        P(("dom", "blk"), None),
        P(("dom", "blk")),
    )
    out_specs = (P("blk", "dom"), P("blk"), P(("dom", "blk")))
    return jax.shard_map(body, mesh=mesh, in_specs=in_specs, out_specs=out_specs, check_vma=False)
```

```python
import functools
import jax
import jax.numpy as jnp
from jax import lax
from jax.experimental import pallas as pl
from jax.experimental.pallas import tpu as pltpu
from jax.sharding import PartitionSpec as P

ROTS = 36
LANES = 128
F32 = jnp.float32
BF16 = jnp.bfloat16
LOW = -3.0e38
VMEM_BYTES = 24 * 1024 * 1024


def offsets(blk):
    half = blk // 2
    first = list(range(half, blk - 1)) + [0]
    second = [blk - 1] + list(range(half - 1, 0, -1))
    pairs = list(zip(first, second))
    order = list(zip(range(half), [0, *range(2, half), 1]))
    order = order[1:] + order[:1]
    return pairs, order


def routed(block, dom, blk, move):
    pairs = []
    for d in range(dom):
        for b in range(blk):
            to = move(d, b)
            if to is not None:
                pairs.append((d * blk + b, to[0] * blk + to[1]))
    return lax.ppermute(block, ("dom", "blk"), pairs)


def call(kernel, outs, args, scratch=(), flops=1_000_000):
    total = sum(a.size * a.dtype.itemsize for a in args) + sum(o.size * o.dtype.itemsize for o in outs)
    near = pl.BlockSpec(memory_space=pltpu.VMEM)
    return pl.pallas_call(
        kernel,
        out_shape=tuple(outs),
        in_specs=[near] * len(args),
        out_specs=tuple([near] * len(outs)),
        scratch_shapes=list(scratch),
        compiler_params=pltpu.CompilerParams(vmem_limit_bytes=VMEM_BYTES),
        cost_estimate=pl.CostEstimate(flops=flops, bytes_accessed=total, transcendentals=0),
    )(*args)


def stack_kernel(own, other, out):
    rows, pixels = own.shape
    step = pixels // ROTS
    for q in range(ROTS):
        base = q * 2 * rows
        out[base : base + rows, :] = own[:, q * step : (q + 1) * step]
        out[base + rows : base + 2 * rows, :] = other[:, q * step : (q + 1) * step]


def pick_offset(core, pair):
    return jnp.where(core == 0, pair[0], pair[1])


def lanes_of(own, other):
    return jnp.concatenate([own, other, own, other], axis=1)


def correlate(recv, stacked, tiles):
    width, pixels = recv[0].shape
    step = pixels // ROTS
    total = stacked.shape[0]
    columns = total // LANES
    rows = ROTS * width
    norms = []
    for t, ref in enumerate(recv):
        block = ref[...].astype(F32)
        norms.append(0.5 * jnp.sum(block * block, axis=1, keepdims=True))
        for u in range(ROTS // 4):
            tile = jnp.concatenate([block[:, (4 * u + a) * step : (4 * u + a + 1) * step] for a in range(4)], axis=0)
            tiles[t * rows + 16 * u : t * rows + 16 * (u + 1), :] = tile.astype(BF16)
    sums = [[None] * columns for _ in recv]
    for n in range(columns // 2):
        weights = stacked[n * 256 : (n + 1) * 256, :]
        got = lax.dot_general(tiles[...], weights, (((1,), (1,)), ((), ())), preferred_element_type=F32)
        for t, held in enumerate(sums):
            for m in range(-1, columns):
                part = None
                if m >= 0:
                    part = got[t * rows + 8 * m : t * rows + 8 * m + 8, :LANES]
                if m + 1 < columns:
                    extra = got[t * rows + 8 * m + 8 : t * rows + 8 * m + 16, LANES:]
                    part = extra if part is None else part + extra
                place = (2 * n - m) % columns
                held[place] = part if held[place] is None else held[place] + part
    corr = []
    for held in sums:
        whole = jnp.concatenate(held, axis=1)
        corr.append(whole[:4, :] + pltpu.roll(whole, total - 64, 1)[4:, :])
    return jnp.concatenate(corr, axis=0), jnp.concatenate(norms, axis=0)


def early_kernel(*refs):
    recv, (stacked, corr, norm, tiles) = refs[:-4], refs[-4:]
    value, norms = correlate(recv, stacked, tiles)
    corr[...] = value
    norm[...] = jnp.broadcast_to(norms, norm.shape)


def forward_kernel(pairs, *refs):
    recv, (stacked, lists_own, lists_other) = refs[:-9], refs[-9:-6]
    early, early_norm, exps, stats, tiles, corr = refs[-6:]
    core = lax.axis_index("dom") & 1
    spot = lax.axis_index("blk")
    width = recv[0].shape[0]
    slots = lists_own.shape[0] // 2
    columns = stacked.shape[0] // LANES
    late, late_norm = correlate(recv, stacked, tiles)
    corr[: early.shape[0], :] = early[...]
    corr[early.shape[0] :, :] = late
    norm = jnp.concatenate([early_norm[...], jnp.broadcast_to(late_norm, (late_norm.shape[0], LANES))], axis=0)
    lists = lanes_of(lists_own[...], lists_other[...])
    inverse = lists[slots : slots + 1, :]
    ids = jnp.concatenate(
        [
            lax.broadcasted_iota(jnp.int32, (width, LANES), 0) + (spot ^ pick_offset(core, pair)) * width
            for pair in pairs
        ],
        axis=0,
    ).astype(F32)
    mask = lists[0:1, :] == ids
    for s in range(1, slots):
        mask = mask | (lists[s : s + 1, :] == ids)
    scores = [inverse * (corr[:, c * LANES : (c + 1) * LANES] - norm) for c in range(columns)]
    peak = jnp.full(ids.shape, LOW, F32)
    for score in scores:
        peak = jnp.maximum(peak, score)
    peak = jnp.max(jnp.where(mask, peak, LOW), axis=0, keepdims=True)
    peak = jnp.maximum(peak, pltpu.roll(peak, 64, 1))
    mass = jnp.zeros(ids.shape, F32)
    for c, score in enumerate(scores):
        term = jnp.where(mask, jnp.exp(score - peak), 0.0)
        exps[:, c * LANES : (c + 1) * LANES] = term
        mass = mass + term
    mass = jnp.sum(mass, axis=0, keepdims=True)
    mass = mass + pltpu.roll(mass, 64, 1)
    stats[...] = jnp.concatenate([peak, mass, jnp.zeros((6, LANES), F32)], axis=0)


def backward_kernel(pairs, order, *refs):
    taken = range(len(pairs))
    core = lax.axis_index("dom") & 1
    exps, mine, theirs, stacked = refs[:4]
    sends, (own, evidence, left) = refs[4:-3], refs[-3:]
    total = stacked.shape[0]
    columns = total // LANES
    width = exps.shape[0] // len(pairs)
    rows = ROTS * width
    extra_rows, step = sends[0].shape[0] - rows, sends[0].shape[1]
    peak, mass = mine[0:1, :], mine[1:2, :]
    peak_far, mass_far = pltpu.roll(theirs[0:1, :], 32, 1), pltpu.roll(theirs[1:2, :], 32, 1)
    top = jnp.maximum(peak, peak_far)
    share = jnp.exp(peak - top)
    whole = mass * share + mass_far * jnp.exp(peak_far - top)
    factor = share / whole
    evidence[...] = (top + jnp.log(whole))[:, : evidence.shape[1]]
    weights = []
    for n, t in enumerate(taken):
        post = jnp.concatenate(
            [exps[width * t : width * (t + 1), c * LANES : (c + 1) * LANES] * factor for c in range(columns)], axis=1
        )
        weights.append(jnp.sum(post, axis=1, keepdims=True))
        two = jnp.concatenate([post, pltpu.roll(post, 64, 1)], axis=0)
        four = jnp.concatenate([two, pltpu.roll(two, 128, 1)], axis=0).astype(BF16)
        for u in range(ROTS // 4):
            cut = total - 256 * u
            rotated = four if u == 0 else jnp.concatenate([four[:, cut:], four[:, :cut]], axis=1)
            left[n * rows + 16 * u : n * rows + 16 * (u + 1), :] = rotated
    result = jnp.dot(left[...], stacked[...], preferred_element_type=F32)
    lane = lax.broadcasted_iota(jnp.int32, (extra_rows, step), 1)
    blocks = []
    for t in taken:
        piece = jnp.concatenate([weights[t], jnp.zeros((extra_rows - width, 1), F32)], axis=0)
        block = result[t * rows : (t + 1) * rows, :]
        high = piece.astype(BF16).astype(F32)
        middle = (piece - high).astype(BF16).astype(F32)
        low = piece - high - middle
        if pairs[t][0] == 0:
            own[:rows, :] = block
            own[rows:, :] = jnp.where(lane == 0, piece, 0.0)
        tail = jnp.where(lane == 0, high, jnp.where(lane == 1, middle, jnp.where(lane == 2, low, 0.0)))
        blocks.append(jnp.concatenate([block, tail], axis=0))
    for send, (i, j) in zip(sends, order):
        send[...] = (blocks[i] if i == j else jnp.where(core == 0, blocks[i], blocks[j])).astype(BF16)


def gather_kernel(pairs, width, *refs):
    turns = len(pairs)
    own, recv, outs, split = refs[0], refs[1 : 1 + turns], refs[1 + turns : -1], refs[-1]
    me = lax.axis_index("dom")
    core = me & 1
    rows = ROTS * width
    value = None
    for t in range(turns):
        block = recv[t][...].astype(F32)
        if pairs[t][0] == 0:
            block = jnp.where(core == 0, own[...], block)
        value = block if value is None else value + block
    weight = jnp.sum(value[rows : rows + width, :], axis=1, keepdims=True)
    weight = jnp.broadcast_to(weight, (width, value.shape[1]))
    shards = len(outs)
    part = rows // shards
    for s in range(shards):
        split[s, :, :] = jnp.concatenate([value[s * part : (s + 1) * part, :], weight], axis=0)
    for s in range(shards):
        outs[s][...] = split[me ^ s]


def finish_kernel(width, *refs):
    parts, (sums, weights) = refs[:-2], refs[-2:]
    value = parts[0][...]
    for part in parts[1:]:
        value = value + part[...]
    step = value.shape[1]
    chunks = value.shape[0] // width - 1
    for c in range(chunks):
        sums[:, c * step : (c + 1) * step] = value[c * width : (c + 1) * width, :]
    tail = value[chunks * width :, :LANES]
    pick = lax.broadcasted_iota(jnp.int32, tail.shape, 0) == lax.broadcasted_iota(jnp.int32, tail.shape, 1)
    weights[...] = jnp.sum(jnp.where(pick, tail, 0.0), axis=0, keepdims=True)[:, : weights.shape[1]]


def body(particles, references, inv_noise, significant, sig_count):
    dom, blk = lax.axis_size("dom"), lax.axis_size("blk")
    count, pixels = particles.shape
    width = references.shape[0]
    slots = significant.shape[1]
    step = pixels // ROTS
    pairs, order = offsets(blk)
    turns = len(pairs)
    total = ROTS * 2 * count
    shape = jax.ShapeDtypeStruct

    def over_blk(block, pair):
        def move(d, b):
            by = pair[d & 1]
            return None if by == 0 else (d, b ^ by)

        return routed(block, dom, blk, move)

    def shared(block, pair):
        def move(d, b):
            if pair[0] != 0:
                return (d, b ^ pair[d & 1])
            return (d ^ 1, b) if d & 1 else (d ^ 1, b ^ pair[1])

        return routed(block, dom, blk, move)

    def over_dom(block, by):
        return routed(block, dom, blk, lambda d, b: (d ^ by, b))

    other = over_dom(particles, 1)
    row = lax.broadcasted_iota(jnp.int32, (2 * slots, count), 0)
    named = jnp.pad(significant.T, ((0, slots), (0, 0)))
    named = jnp.where(row < sig_count[None, :], named, -1).astype(F32)
    lists = jnp.where(row < slots, named, inv_noise[None, :])
    recv = [shared(references, pair) for pair in pairs]
    lists_other = over_dom(lists, 1)
    (stacked,) = call(stack_kernel, [shape((total, step), BF16)], [particles, other])
    rows = ROTS * width

    def buffers(blocks):
        return [pltpu.VMEM((blocks * rows, step), BF16)]

    early = turns // 2
    corr, norm = call(
        early_kernel,
        [shape((early * width, total), F32), shape((early * width, LANES), F32)],
        [*recv[:early], stacked],
        buffers(early),
        flops=2 * early * rows * step * total,
    )
    exps, stats = call(
        functools.partial(forward_kernel, pairs),
        [shape((turns * width, total), F32), shape((8, LANES), F32)],
        [*recv[early:], stacked, lists, lists_other, corr, norm],
        buffers(turns - early) + [pltpu.VMEM((turns * width, total), F32)],
        flops=2 * (turns - early) * rows * step * total,
    )
    stats_other = over_dom(stats, 1)
    message = shape((rows + 8, step), BF16)
    *sends, own, evidence = call(
        functools.partial(backward_kernel, pairs, order),
        [message] * turns + [shape((rows + 8, step), F32), shape((1, count), F32)],
        [exps, stats, stats_other, stacked],
        [pltpu.VMEM((turns * rows, total), BF16)],
        flops=2 * turns * rows * step * total,
    )
    ways = [(pairs[i][0], pairs[j][1]) for i, j in order]
    recv = [over_blk(send, way) for send, way in zip(sends, ways)]
    part = rows // dom + width
    parts = call(
        functools.partial(gather_kernel, ways, width),
        [shape((part, step), F32)] * dom,
        [own, *recv],
        [pltpu.VMEM((dom, part, step), F32)],
    )
    parts = [parts[0]] + [over_dom(parts[s], s) for s in [*range(2, dom), 1]]
    sums, weights = call(
        functools.partial(finish_kernel, width),
        [shape((width, pixels // dom), F32), shape((1, width), F32)],
        parts,
    )
    return sums, weights.reshape(width), evidence.reshape(count)


def solution(mesh):
    in_specs = (
        P(("dom", "blk"), None),
        P("blk", None),
        P(("dom", "blk")),
        P(("dom", "blk"), None),
        P(("dom", "blk")),
    )
    out_specs = (P("blk", "dom"), P("blk"), P(("dom", "blk")))
    return jax.shard_map(body, mesh=mesh, in_specs=in_specs, out_specs=out_specs, check_vma=False)
```
